32 devices in a mesh: rows: 8 (over z, y), feat: 4 (over x, core).
Axes of the slice: x: 2, y: 2, z: 4, core: 2. Of those that a mesh axis runs over, the one named last changes fastest.
Arguments:
- acts: bfloat16 [8192, 8192], P('rows', 'feat'), may hold values from -6 to 6
- out_grads: bfloat16 [8192, 8192], P('rows', 'feat'), may hold values from -6 to 6
- proj_in: bfloat16 [8192, 256], P('feat'), may hold values from -0.0625 to 0.0625
- proj_out: bfloat16 [8192, 256], P('feat'), may hold values from -0.0625 to 0.0625
- assignment: int32 [8192], P('rows'), may hold values from 0 to 255
- codes: int32 [1024, 65536], P('rows', 'feat'), may hold values from -128 to 127
- zero_points: int32 [65536], P('feat'), may hold values from -64 to 63
- scales: float32 [65536], P('feat'), may hold values from 2e-06 to 2e-05
Outputs:
- scores: float32 [256, 1024], P('feat', 'rows')
The draws below stay inside these ranges and needn't reach their ends.
All inputs are finite; a program needn't handle non-finite values.
Results may differ from the reference program's by a relative error of at most 0.005.
Values may be sent and summed in bfloat16 or wider, within the bound.
A program may use at most 128 MiB of HBM per device.

```python
import math
import jax
import jax.numpy as jnp
from jax import lax

D = 8192
RANK = 256
QUERIES = 256
TOK_DEV = 1024
STORE_DEV = 128
TOKENS = 8192
NSTORE = 1024
FEATURES = 65536
N_ROWS = 8


def with_ends(drawn, stream_key, low, largest):
    spot = [jax.random.randint(jax.random.fold_in(stream_key, axis), (), 0, length) for axis, length in enumerate(drawn.shape)]
    longest = drawn.shape.index(max(drawn.shape))
    beside = spot[:longest] + [(spot[longest] + 1) % drawn.shape[longest]] + spot[longest + 1:]
    return drawn.at[tuple(spot)].set(low).at[tuple(beside)].set(largest)


def block_levels(stream_key, dims, split, least, largest):
    loudness = 1.0
    for position, blocks in split:
        draws = jax.random.uniform(jax.random.fold_in(jax.random.fold_in(stream_key, 6), position), (blocks,), jnp.float32, least / len(split), largest / len(split))
        loudness = loudness * jnp.repeat(jnp.exp(draws), dims[position] // blocks).reshape((-1,) + (1,) * (len(dims) - 1 - position))
    return loudness


def centred(key, shape, width, reach, split=(), kind=jnp.bfloat16):
    gain = block_levels(key, shape, split, -0.22, 0.18) if split else 1.0
    array = jax.random.normal(key, shape, jnp.float32) * width * gain
    return jnp.minimum(jnp.maximum(array, -reach), reach).astype(kind)


def setup_inputs(seed: int = 0) -> dict:
    streams_of = jax.random.split(jax.random.key(seed), 9)
    return {
        "acts": centred(streams_of[0], (TOKENS, D), 1.0, 6.0, ((0, 8), (1, 4))),
        "out_grads": centred(streams_of[1], (TOKENS, D), 1.0, 6.0, ((0, 8), (1, 4))),
        "proj_in": centred(streams_of[2], (D, RANK), D ** -0.5, 0.0625, ((0, 4),)),
        "proj_out": centred(streams_of[3], (D, RANK), D ** -0.5, 0.0625, ((0, 4),)),
        "assignment": with_ends(jax.random.randint(streams_of[4], (TOKENS,), 0, QUERIES), jax.random.fold_in(streams_of[4], 1), 0, QUERIES - 1).astype(jnp.int32),
        "codes": with_ends(jax.random.randint(streams_of[5], (NSTORE, FEATURES), -128, 128), jax.random.fold_in(streams_of[5], 1), -128, 127).astype(jnp.int32),
        "zero_points": with_ends(jax.random.randint(streams_of[6], (FEATURES,), -64, 64), jax.random.fold_in(streams_of[6], 1), -64, 63).astype(jnp.int32),
        "scales": jnp.clip(jnp.exp(math.log(1.9999999494757503e-05) - 2.3025851 * jax.random.uniform(streams_of[7], (FEATURES,), jnp.float32) ** block_levels(streams_of[7], (FEATURES,), ((0, 4),), -0.2, 0.2)), 1.9999999949504854e-06, 1.9999999494757503e-05),
    }


def reference(acts, out_grads, proj_in, proj_out, assignment, codes, zero_points, scales):
    inner = jnp.dot(acts, proj_in, preferred_element_type=jnp.float32).astype(jnp.bfloat16)
    outer = jnp.dot(out_grads, proj_out, preferred_element_type=jnp.float32).astype(jnp.bfloat16)
    blocks = TOKENS // TOK_DEV

    def accumulate(carry, index):
        start = (index * TOK_DEV).astype(jnp.int32)
        inner_block = lax.dynamic_slice_in_dim(inner, start, TOK_DEV, 0).astype(jnp.float32)
        outer_block = lax.dynamic_slice_in_dim(outer, start, TOK_DEV, 0).astype(jnp.float32)
        owners = lax.dynamic_slice_in_dim(assignment, start, TOK_DEV, 0)
        product = (outer_block[:, :, None] * inner_block[:, None, :]).reshape(TOK_DEV, RANK * RANK)
        return carry + jax.ops.segment_sum(product, owners, num_segments=QUERIES), None

    start_grads = jnp.zeros((QUERIES, RANK * RANK), jnp.float32)
    query_grads, unused = lax.scan(accumulate, start_grads, jnp.arange(blocks, dtype=jnp.int32))
    scaled = (query_grads * scales[None, :]).astype(jnp.bfloat16)
    store_blocks = codes.reshape(N_ROWS, STORE_DEV, RANK * RANK)

    def score_block(block_codes):
        levels = (block_codes - zero_points[None, :]).astype(jnp.bfloat16)
        return lax.dot_general(scaled, levels, (((1,), (1,)), ((), ())), preferred_element_type=jnp.float32)

    parts = lax.map(score_block, store_blocks)
    return jnp.transpose(parts, (1, 0, 2)).reshape(QUERIES, NSTORE)
```

```python
import functools
import jax
import jax.numpy as jnp
from jax import lax
from jax.experimental import pallas as pl
from jax.experimental.pallas import tpu as pltpu
from jax.sharding import PartitionSpec as P

QUERIES = 256
GROUP = 16
WINDOW = 96
ALIGN = 16
LANES = 128
MESH = pl.DeviceIdType.MESH


def exchange_kernel(nr, nf, inner_ref, outer_ref, in_all, out_all, rin, rout,
                    rs_send, rs_recv, ring_send, ring_recv, f_send, f_recv, g_send, g_recv):
    row = lax.axis_index("rows")
    me = lax.axis_index("feat")
    tq = rin.shape[1]
    odd = lax.rem(row, 2)
    pos = (1 - odd) * (row // 2) + odd * (nr - 1 - row // 2)

    def row_at(p):
        p = lax.rem(p + 2 * nr, nr)
        back = p // (nr // 2)
        return (1 - back) * (2 * p) + back * (2 * (nr - 1 - p) + 1)

    right, left = row_at(pos + 1), row_at(pos - 1)
    core = me + 1 - 2 * lax.rem(me, 2)
    half = nf // 2

    barrier = pltpu.get_barrier_semaphore()
    for d in range(1, nf):
        pl.semaphore_signal(barrier, inc=1, device_id=(row, lax.rem(me + d, nf)), device_id_type=MESH)
    for r in (right, left):
        pl.semaphore_signal(barrier, inc=1, device_id=(r, me), device_id_type=MESH)
    pl.semaphore_wait(barrier, nf + 1)

    def remote(src, dst, ssem, rsem, dev):
        return pltpu.make_async_remote_copy(
            src_ref=src, dst_ref=dst, send_sem=ssem, recv_sem=rsem, device_id=dev, device_id_type=MESH)

    sends = []
    firsts = []
    for d in range(1, nf):
        to = lax.rem(me + d, nf)
        a = remote(inner_ref.at[to], rin.at[d - 1], rs_send.at[0, d - 1], rs_recv.at[0, d - 1], (row, to))
        b = remote(outer_ref.at[to], rout.at[d - 1], rs_send.at[1, d - 1], rs_recv.at[1, d - 1], (row, to))
        a.start()
        b.start()
        firsts.append((a, b))
        sends += [a, b]
    si = inner_ref[me].astype(jnp.float32)
    for a, b in firsts:
        a.wait_recv()
    for d in range(1, nf):
        si += rin[d - 1].astype(jnp.float32)
    mine = pl.ds(pl.multiple_of(me * tq, tq), tq)
    in_all[row, mine, :] = si.astype(jnp.bfloat16)
    for a, b in firsts:
        b.wait_recv()
    so = outer_ref[me].astype(jnp.float32)
    for d in range(1, nf):
        so += rout[d - 1].astype(jnp.float32)
    out_all[row] = so.astype(jnp.bfloat16)

    steps_r = nr // 2
    steps_l = nr - 1 - steps_r

    def chunk_row(e):
        return row_at(pos - e) if e <= steps_r else row_at(pos + e - steps_r)

    def ring_copies(e, to, sem):
        r = chunk_row(e)
        return (remote(in_all.at[r, mine], in_all.at[r, mine], ring_send.at[0, sem], ring_recv.at[0, sem], (to, me)),
                remote(out_all.at[r], out_all.at[r], ring_send.at[1, sem], ring_recv.at[1, sem], (to, me)))

    def launch(e, to, sem):
        pair = ring_copies(e, to, sem)
        for c in pair:
            c.start()
            sends.append(c)
        return pair

    tails = []
    feats = {}

    def spread(e):
        r = chunk_row(e)
        block = in_all.at[r, mine]
        got = []
        for d in range(1, half):
            c = remote(block, block, f_send.at[e, d], f_recv.at[e, d], (row, lax.rem(me + 2 * d, nf)))
            c.start()
            sends.append(c)
            got.append(c)
        c = remote(block, block, f_send.at[e, 0], f_recv.at[e, 0], (row, core))
        c.start()
        sends.append(c)
        tails.append(c)
        feats[e] = got

    def pass_on(e):
        r = chunk_row(e)
        for d in range(1, half):
            feats[e][d - 1].wait_recv()
            src = lax.rem(me + nf - 2 * d, nf)
            block = in_all.at[r, pl.ds(pl.multiple_of(src * tq, tq), tq)]
            c = remote(block, block, g_send.at[e, d], g_recv.at[e, d], (row, core))
            c.start()
            sends.append(c)
            tails.append(c)

    cr = launch(0, right, 0)
    cl = launch(0, left, steps_r) if steps_l else None
    spread(0)
    late = [0]
    for s in range(steps_r):
        e = 1 + s
        fresh = [e]
        nxt = None
        cr[0].wait_recv()
        cr[1].wait_recv()
        if s + 1 < steps_r:
            nxt = launch(e, right, s + 1)
        spread(e)
        cr = nxt
        if s < steps_l:
            e = 1 + steps_r + s
            cl[0].wait_recv()
            cl[1].wait_recv()
            nxt = None
            if s + 1 < steps_l:
                nxt = launch(e, left, steps_r + s + 1)
            spread(e)
            cl = nxt
            fresh.append(e)
        for e in late:
            pass_on(e)
        late = fresh
    for e in late:
        pass_on(e)
    for c in tails:
        c.wait_recv()
    for c in sends:
        c.wait_send()


def grads_kernel(starts_ref, inner_ref, outer_ref, scales_ref, out_ref, in_w, out_w, acc):
    g = pl.program_id(0)
    nr, tokens, rank = inner_ref.shape
    local_rank = scales_ref.shape[0]
    begins = []
    loops = jnp.int32(1)
    for r in range(nr):
        begin = starts_ref[r, g] // ALIGN * ALIGN
        begins.append(begin)
        loops = jnp.maximum(loops, (starts_ref[r, g + 1] - begin + WINDOW - 1) // WINDOW)
    acc[...] = jnp.zeros_like(acc)
    ids_here = (g * GROUP + lax.broadcasted_iota(jnp.int32, (GROUP, 1), 0)).astype(jnp.float32)
    line = lax.broadcasted_iota(jnp.int32, (WINDOW, 1), 0)

    def one(k, carry):
        for r in range(nr):
            want = begins[r] + k * WINDOW
            at = pl.multiple_of(jnp.minimum(want, tokens - WINDOW), ALIGN)
            here = pl.ds(r * WINDOW, WINDOW)
            in_w[here, :] = inner_ref[r, pl.ds(at, WINDOW), :]
            rows = outer_ref[r, pl.ds(at, WINDOW), :].astype(jnp.float32)
            out_w[here, :] = jnp.where(line >= want - at, rows, 0.0)
        turned = out_w[...].T
        mask = turned[local_rank:local_rank + 1, :] == ids_here
        spread = jnp.where(mask[None], turned[:local_rank, None, :], 0.0).astype(jnp.bfloat16)
        spread = spread.reshape(local_rank * GROUP, in_w.shape[0])
        acc[...] += jnp.dot(spread, in_w[...], preferred_element_type=jnp.float32)
        return carry

    lax.fori_loop(0, loops, one, 0)
    grads = acc[...].reshape(local_rank, GROUP, rank)
    out_ref[...] = (grads * scales_ref[...][:, None, :]).astype(jnp.bfloat16)


def score_kernel(grads_ref, codes_ref, zero_ref, out_ref):
    @pl.when(pl.program_id(0) == 0)
    def _():
        out_ref[...] = jnp.zeros_like(out_ref)

    width = grads_ref.shape[2]
    total = out_ref[...]
    for i in range(grads_ref.shape[0]):
        cols = slice(i * width, (i + 1) * width)
        levels = (codes_ref[:, cols] - zero_ref[:, cols]).astype(jnp.float32).astype(jnp.bfloat16)
        total += lax.dot_general(grads_ref[i], levels, (((1,), (1,)), ((), ())),
                                 preferred_element_type=jnp.float32)
    out_ref[...] = total


def local(nr, nf, acts, out_grads, proj_in, proj_out, assignment, codes, zero_points, scales):
    tokens = acts.shape[0]
    rank = proj_in.shape[1]
    local_rank = rank // nf
    bf = jnp.bfloat16
    part_inner = jnp.dot(acts, proj_in, preferred_element_type=jnp.float32).astype(bf)
    part_outer = jnp.dot(out_grads, proj_out, preferred_element_type=jnp.float32).astype(bf)

    order = lax.iota(jnp.int32, tokens)
    key = assignment * tokens + order
    place = jnp.sum((key[:, None] < key[None, :]).astype(jnp.int32), axis=0)
    sorter = (place[None, :] == order[:, None]).astype(bf)
    both = jnp.dot(sorter, jnp.concatenate([part_inner, part_outer], 1), preferred_element_type=jnp.float32)
    inner = both[:, :rank].astype(bf).reshape(nf, tokens // nf, rank)
    ids = jnp.sum(jnp.where(place[None, :] == order[:, None], assignment[None, :], 0), axis=1)
    ids = jnp.where(lax.axis_index("feat") == 0, ids, 0).astype(bf)
    outer = both[:, rank:].astype(bf).reshape(tokens, nf, local_rank).transpose(1, 0, 2)
    wide = -(-(local_rank + 1) // LANES) * LANES
    outer = jnp.concatenate([
        outer,
        jnp.broadcast_to(ids[None, :, None], (nf, tokens, 1)),
        jnp.zeros((nf, tokens, wide - local_rank - 1), bf)], 2)
    edges = lax.iota(jnp.int32, QUERIES // GROUP + 1) * GROUP
    starts = jnp.sum((assignment[None, :] < edges[:, None]).astype(jnp.int32), axis=1)
    starts = lax.all_gather(starts, "rows")

    vmem = pl.BlockSpec(memory_space=pltpu.VMEM)
    dma = pltpu.SemaphoreType.DMA
    in_all, out_all = pl.pallas_call(
        functools.partial(exchange_kernel, nr, nf),
        out_shape=(jax.ShapeDtypeStruct((nr, tokens, rank), bf), jax.ShapeDtypeStruct((nr, tokens, wide), bf)),
        in_specs=[vmem, vmem],
        out_specs=(vmem, vmem),
        scratch_shapes=[
            pltpu.VMEM((nf - 1, tokens // nf, rank), bf),
            pltpu.VMEM((nf - 1, tokens, wide), bf),
            dma((2, nf - 1)), dma((2, nf - 1)),
            dma((2, nr)), dma((2, nr)),
            dma((nr, nf // 2)), dma((nr, nf // 2)),
            dma((nr, nf // 2)), dma((nr, nf // 2)),
        ],
        compiler_params=pltpu.CompilerParams(
            collective_id=0, has_side_effects=True, vmem_limit_bytes=48 * 2 ** 20),
    )(inner, outer)

    grads = pl.pallas_call(
        grads_kernel,
        out_shape=jax.ShapeDtypeStruct((local_rank, QUERIES, rank), bf),
        grid=(QUERIES // GROUP,),
        in_specs=[pl.BlockSpec(memory_space=pltpu.SMEM), vmem, vmem, vmem],
        out_specs=pl.BlockSpec((local_rank, GROUP, rank), lambda g: (0, g, 0)),
        scratch_shapes=[
            pltpu.VMEM((nr * WINDOW, rank), bf),
            pltpu.VMEM((nr * WINDOW, wide), jnp.float32),
            pltpu.VMEM((local_rank * GROUP, rank), jnp.float32),
        ],
        compiler_params=pltpu.CompilerParams(vmem_limit_bytes=56 * 2 ** 20),
    )(starts, in_all, out_all, scales.reshape(local_rank, rank))

    stored, features = codes.shape
    step = min(8, local_rank)
    terms = pl.pallas_call(
        score_kernel,
        out_shape=jax.ShapeDtypeStruct((QUERIES, stored), jnp.float32),
        grid=(local_rank // step,),
        in_specs=[
            pl.BlockSpec((step, QUERIES, rank), lambda i: (i, 0, 0)),
            pl.BlockSpec((stored, step * rank), lambda i: (0, i)),
            pl.BlockSpec((1, step * rank), lambda i: (0, i)),
        ],
        out_specs=pl.BlockSpec((QUERIES, stored), lambda i: (0, 0)),
        compiler_params=pltpu.CompilerParams(vmem_limit_bytes=32 * 2 ** 20),
    )(grads, codes, zero_points.reshape(1, features))
    return lax.psum_scatter(terms, "feat", scatter_dimension=0, tiled=True)


def solution(mesh):
    in_specs = (
        P("rows", "feat"),
        P("rows", "feat"),
        P("feat", None),
        P("feat", None),
        P("rows"),
        P("rows", "feat"),
        P("feat"),
        P("feat"),
    )
    out_specs = P("feat", "rows")
    body = functools.partial(local, mesh.shape["rows"], mesh.shape["feat"])
    return jax.shard_map(body, mesh=mesh, in_specs=in_specs, out_specs=out_specs, check_vma=False)
```

```python
import functools
import jax
import jax.numpy as jnp
from jax import lax
from jax.experimental import pallas as pl
from jax.experimental.pallas import tpu as pltpu
from jax.sharding import PartitionSpec as P

QUERIES = 256
GROUP = 16
WINDOW = 96
ALIGN = 16
LANES = 128
MESH = pl.DeviceIdType.MESH


def exchange_kernel(nr, nf, local_rank, inner_ref, outer_ref, ids_ref, in_all, out_all,
                    rin, rout, far_in, far_out, to_in, to_out, rs_send, rs_recv, far_send, far_recv,
                    ring_send, ring_recv, f_send, f_recv, g_send, g_recv):
    row = lax.axis_index("rows")
    me = lax.axis_index("feat")
    tq, wide = rin.shape[1], rout.shape[2]
    odd = lax.rem(row, 2)
    pos = (1 - odd) * (row // 2) + odd * (nr - 1 - row // 2)

    def row_at(p):
        p = lax.rem(p + 2 * nr, nr)
        back = p // (nr // 2)
        return (1 - back) * (2 * p) + back * (2 * (nr - 1 - p) + 1)

    right, left = row_at(pos + 1), row_at(pos - 1)
    core = me + 1 - 2 * lax.rem(me, 2)
    half = nf // 2

    barrier = pltpu.get_barrier_semaphore()
    for d in range(1, half):
        pl.semaphore_signal(barrier, inc=1, device_id=(row, lax.rem(me + 2 * d, nf)), device_id_type=MESH)
    pl.semaphore_signal(barrier, inc=1, device_id=(row, core), device_id_type=MESH)
    for r in (right, left):
        pl.semaphore_signal(barrier, inc=1, device_id=(r, me), device_id_type=MESH)
    pl.semaphore_wait(barrier, half + 2)

    def remote(src, dst, ssem, rsem, dev):
        return pltpu.make_async_remote_copy(
            src_ref=src, dst_ref=dst, send_sem=ssem, recv_sem=rsem, device_id=dev, device_id_type=MESH)

    sends = []

    def begin(*args):
        c = remote(*args)
        c.start()
        sends.append(c)
        return c

    lane = lax.broadcasted_iota(jnp.int32, (1, wide), 1)

    def unpack(packed):
        both = packed.astype(jnp.float32)
        return both + pltpu.roll(both, wide - local_rank, 1)

    def pack(total):
        high = total.astype(jnp.bfloat16).astype(jnp.float32)
        low = pltpu.roll(total - high, local_rank, 1)
        return jnp.where(lane < local_rank, high, low).astype(jnp.bfloat16)

    near = {}
    for d in list(range(1, half)) + [0]:
        to = lax.rem(core + 2 * d, nf)
        near[d] = (begin(inner_ref.at[to], rin.at[d], rs_send.at[0, d], rs_recv.at[0, d], (row, core)),
                   begin(outer_ref.at[to], rout.at[d], rs_send.at[1, d], rs_recv.at[1, d], (row, core)))
    far = {}
    for d in range(1, half):
        to = lax.rem(me + 2 * d, nf)
        near[d][0].wait_recv()
        to_in[d - 1] = inner_ref[to] + rin[d]
        one = begin(to_in.at[d - 1], far_in.at[d - 1], far_send.at[0, d], far_recv.at[0, d], (row, to))
        near[d][1].wait_recv()
        to_out[d - 1] = pack(unpack(outer_ref[to]) + unpack(rout[d]))
        two = begin(to_out.at[d - 1], far_out.at[d - 1], far_send.at[1, d], far_recv.at[1, d], (row, to))
        far[d] = (one, two)
    mine = pl.ds(pl.multiple_of(me * tq, tq), tq)
    near[0][0].wait_recv()
    total = inner_ref[me] + rin[0]
    for d in range(1, half):
        far[d][0].wait_recv()
        total += far_in[d - 1]
    in_all[row, mine, :] = total.astype(jnp.bfloat16)
    near[0][1].wait_recv()
    total = unpack(outer_ref[me]) + unpack(rout[0])
    for d in range(1, half):
        far[d][1].wait_recv()
        total += unpack(far_out[d - 1])
    total = jnp.where(lane < local_rank, total, jnp.where(lane == local_rank, ids_ref[...], 0.0))
    out_all[row] = total.astype(jnp.bfloat16)

    steps_r = nr // 2
    steps_l = nr - 1 - steps_r

    def chunk_row(e):
        return row_at(pos - e) if e <= steps_r else row_at(pos + e - steps_r)

    def ring_copy(e, to, sem, w):
        r = chunk_row(e)
        block = out_all.at[r] if w else in_all.at[r, mine]
        return remote(block, block, ring_send.at[w, sem], ring_recv.at[w, sem], (to, me))

    def launch(e, to, sem, which=(0, 1)):
        pair = [ring_copy(e, to, sem, w) for w in which]
        for c in pair:
            c.start()
            sends.append(c)
        return pair

    tails = []
    feats = {}

    def spread(e):
        r = chunk_row(e)
        block = in_all.at[r, mine]
        got = []
        for d in range(1, half):
            c = remote(block, block, f_send.at[e, d], f_recv.at[e, d], (row, lax.rem(me + 2 * d, nf)))
            c.start()
            sends.append(c)
            got.append(c)
        c = remote(block, block, f_send.at[e, 0], f_recv.at[e, 0], (row, core))
        c.start()
        sends.append(c)
        tails.append(c)
        feats[e] = got

    def pass_on(e):
        r = chunk_row(e)
        for d in range(1, half):
            feats[e][d - 1].wait_recv()
            src = lax.rem(me + nf - 2 * d, nf)
            block = in_all.at[r, pl.ds(pl.multiple_of(src * tq, tq), tq)]
            c = remote(block, block, g_send.at[e, d], g_recv.at[e, d], (row, core))
            c.start()
            sends.append(c)
            tails.append(c)

    cr = launch(0, right, 0)
    cl = launch(0, left, steps_r)
    spread(0)
    late = [0]
    for s in range(steps_r):
        e = 1 + s
        fresh = [e]
        for c in cr:
            c.wait_recv()
        if s + 1 < steps_r:
            cr = launch(e, right, s + 1, (0, 1) if s + 2 < steps_r else (0,))
        spread(e)
        for c in cl:
            c.wait_recv()
        if s < steps_l:
            e = 1 + steps_r + s
            cl = launch(e, left, steps_r + s + 1, (0, 1) if s + 1 < steps_l else (1,))
            spread(e)
            fresh.append(e)
        for e in late:
            pass_on(e)
        late = fresh
    for e in late:
        pass_on(e)
    for c in tails:
        c.wait_recv()
    for c in sends:
        c.wait_send()


def total_kernel(nf, terms_ref, out_ref, got, send, recv):
    row = lax.axis_index("rows")
    me = lax.axis_index("feat")
    count = out_ref.shape[0]
    barrier = pltpu.get_barrier_semaphore()
    for d in range(1, nf):
        pl.semaphore_signal(barrier, inc=1, device_id=(row, lax.rem(me + d, nf)), device_id_type=MESH)
    pl.semaphore_wait(barrier, nf - 1)
    copies = []
    for d in range(1, nf):
        to = lax.rem(me + d, nf)
        c = pltpu.make_async_remote_copy(
            src_ref=terms_ref.at[pl.ds(pl.multiple_of(to * count, count), count)], dst_ref=got.at[d - 1],
            send_sem=send.at[d - 1], recv_sem=recv.at[d - 1], device_id=(row, to), device_id_type=MESH)
        c.start()
        copies.append(c)
    total = terms_ref[pl.ds(pl.multiple_of(me * count, count), count), :]
    for d in range(1, nf):
        copies[d - 1].wait_recv()
        total += got[d - 1]
    out_ref[...] = total
    for c in copies:
        c.wait_send()


def grads_kernel(starts_ref, inner_ref, outer_ref, scales_ref, out_ref, in_w, out_w, acc):
    g = pl.program_id(0)
    nr, tokens, rank = inner_ref.shape
    local_rank = scales_ref.shape[0]
    begins = []
    loops = jnp.int32(1)
    for r in range(nr):
        begin = starts_ref[r, g] // ALIGN * ALIGN
        begins.append(begin)
        loops = jnp.maximum(loops, (starts_ref[r, g + 1] - begin + WINDOW - 1) // WINDOW)
    acc[...] = jnp.zeros_like(acc)
    ids_here = (g * GROUP + lax.broadcasted_iota(jnp.int32, (GROUP, 1), 0)).astype(jnp.float32)
    line = lax.broadcasted_iota(jnp.int32, (WINDOW, 1), 0)

    def one(k, carry):
        for r in range(nr):
            want = begins[r] + k * WINDOW
            at = pl.multiple_of(jnp.minimum(want, tokens - WINDOW), ALIGN)
            here = pl.ds(r * WINDOW, WINDOW)
            in_w[here, :] = inner_ref[r, pl.ds(at, WINDOW), :]
            rows = outer_ref[r, pl.ds(at, WINDOW), :].astype(jnp.float32)
            out_w[here, :] = jnp.where(line >= want - at, rows, 0.0)
        turned = out_w[...].T
        mask = turned[local_rank:local_rank + 1, :] == ids_here
        spread = jnp.where(mask[None], turned[:local_rank, None, :], 0.0).astype(jnp.bfloat16)
        spread = spread.reshape(local_rank * GROUP, in_w.shape[0])
        acc[...] += jnp.dot(spread, in_w[...], preferred_element_type=jnp.float32)
        return carry

    lax.fori_loop(0, loops, one, 0)
    grads = acc[...].reshape(local_rank, GROUP, rank)
    out_ref[...] = (grads * scales_ref[...][:, None, :]).astype(jnp.bfloat16)


def score_kernel(grads_ref, codes_ref, zero_ref, out_ref):
    @pl.when(pl.program_id(0) == 0)
    def _():
        out_ref[...] = jnp.zeros_like(out_ref)

    width = grads_ref.shape[2]
    total = out_ref[...]
    for i in range(grads_ref.shape[0]):
        cols = slice(i * width, (i + 1) * width)
        levels = (codes_ref[:, cols] - zero_ref[:, cols]).astype(jnp.float32).astype(jnp.bfloat16)
        total += lax.dot_general(grads_ref[i], levels, (((1,), (1,)), ((), ())),
                                 preferred_element_type=jnp.float32)
    out_ref[...] = total


def local(nr, nf, acts, out_grads, proj_in, proj_out, assignment, codes, zero_points, scales):
    tokens = acts.shape[0]
    rank = proj_in.shape[1]
    local_rank = rank // nf
    bf = jnp.bfloat16
    parts = [jnp.dot(acts, proj_in, preferred_element_type=jnp.float32),
             jnp.dot(out_grads, proj_out, preferred_element_type=jnp.float32)]

    order = lax.iota(jnp.int32, tokens)
    key = assignment * tokens + order
    place = jnp.sum((key[:, None] < key[None, :]).astype(jnp.int32), axis=0)
    hits = place[None, :] == order[:, None]
    sorter = hits.astype(bf)
    highs = [p.astype(bf) for p in parts]
    lows = [(p - h.astype(jnp.float32)).astype(bf) for p, h in zip(parts, highs)]
    both = jnp.dot(sorter, jnp.concatenate(highs + lows, 1), preferred_element_type=jnp.float32)
    inner = (both[:, :rank] + both[:, 2 * rank:3 * rank]).reshape(nf, tokens // nf, rank)
    ids = jnp.sum(jnp.where(hits, assignment[None, :], 0), axis=1).astype(jnp.float32)[:, None]
    wide = -(-2 * local_rank // LANES) * LANES
    high, low = both[:, rank:2 * rank].astype(bf), both[:, 3 * rank:].astype(bf)
    fill = [jnp.zeros((tokens, wide - 2 * local_rank), bf)] if wide > 2 * local_rank else []
    outer = jnp.stack([
        jnp.concatenate([high[:, i * local_rank:(i + 1) * local_rank],
                         low[:, i * local_rank:(i + 1) * local_rank]] + fill, 1) for i in range(nf)])

    vmem = pl.BlockSpec(memory_space=pltpu.VMEM)
    dma = pltpu.SemaphoreType.DMA
    in_all, out_all = pl.pallas_call(
        functools.partial(exchange_kernel, nr, nf, local_rank),
        out_shape=(jax.ShapeDtypeStruct((nr, tokens, rank), bf), jax.ShapeDtypeStruct((nr, tokens, wide), bf)),
        in_specs=[vmem, vmem, vmem],
        out_specs=(vmem, vmem),
        scratch_shapes=[
            pltpu.VMEM((nf // 2, tokens // nf, rank), jnp.float32),
            pltpu.VMEM((nf // 2, tokens, wide), bf),
            pltpu.VMEM((nf // 2 - 1, tokens // nf, rank), jnp.float32),
            pltpu.VMEM((nf // 2 - 1, tokens, wide), bf),
            pltpu.VMEM((nf // 2 - 1, tokens // nf, rank), jnp.float32),
            pltpu.VMEM((nf // 2 - 1, tokens, wide), bf),
            dma((2, nf // 2)), dma((2, nf // 2)),
            dma((2, nf // 2)), dma((2, nf // 2)),
            dma((2, nr)), dma((2, nr)),
            dma((nr, nf // 2)), dma((nr, nf // 2)),
            dma((nr, nf // 2)), dma((nr, nf // 2)),
        ],
        compiler_params=pltpu.CompilerParams(
            collective_id=0, has_side_effects=True, vmem_limit_bytes=48 * 2 ** 20),
    )(inner, outer, ids)
    edges = lax.iota(jnp.int32, QUERIES // GROUP + 1) * GROUP
    found = out_all[:, :, local_rank].astype(jnp.int32)
    starts = jnp.sum((found[:, None, :] < edges[None, :, None]).astype(jnp.int32), axis=2)

    grads = pl.pallas_call(
        grads_kernel,
        out_shape=jax.ShapeDtypeStruct((local_rank, QUERIES, rank), bf),
        grid=(QUERIES // GROUP,),
        in_specs=[pl.BlockSpec(memory_space=pltpu.SMEM), vmem, vmem, vmem],
        out_specs=pl.BlockSpec((local_rank, GROUP, rank), lambda g: (0, g, 0)),
        scratch_shapes=[
            pltpu.VMEM((nr * WINDOW, rank), bf),
            pltpu.VMEM((nr * WINDOW, wide), jnp.float32),
            pltpu.VMEM((local_rank * GROUP, rank), jnp.float32),
        ],
        compiler_params=pltpu.CompilerParams(vmem_limit_bytes=56 * 2 ** 20),
    )(starts, in_all, out_all, scales.reshape(local_rank, rank))

    stored, features = codes.shape
    step = min(8, local_rank)
    terms = pl.pallas_call(
        score_kernel,
        out_shape=jax.ShapeDtypeStruct((QUERIES, stored), jnp.float32),
        grid=(local_rank // step,),
        in_specs=[
            pl.BlockSpec((step, QUERIES, rank), lambda i: (i, 0, 0)),
            pl.BlockSpec((stored, step * rank), lambda i: (0, i)),
            pl.BlockSpec((1, step * rank), lambda i: (0, i)),
        ],
        out_specs=pl.BlockSpec((QUERIES, stored), lambda i: (0, 0)),
        compiler_params=pltpu.CompilerParams(vmem_limit_bytes=56 * 2 ** 20),
    )(grads, codes, zero_points.reshape(1, features))
    return pl.pallas_call(
        functools.partial(total_kernel, nf),
        out_shape=jax.ShapeDtypeStruct((QUERIES // nf, stored), jnp.float32),
        in_specs=[vmem],
        out_specs=vmem,
        scratch_shapes=[pltpu.VMEM((nf - 1, QUERIES // nf, stored), jnp.float32), dma((nf - 1,)), dma((nf - 1,))],
        compiler_params=pltpu.CompilerParams(collective_id=1, has_side_effects=True),
    )(terms)


def solution(mesh):
    in_specs = (
        P("rows", "feat"),
        P("rows", "feat"),
        P("feat", None),
        P("feat", None),
        P("rows"),
        P("rows", "feat"),
        P("feat"),
        P("feat"),
    )
    out_specs = P("feat", "rows")
    body = functools.partial(local, mesh.shape["rows"], mesh.shape["feat"])
    return jax.shard_map(body, mesh=mesh, in_specs=in_specs, out_specs=out_specs, check_vma=False)
```

```python
import functools
import jax
import jax.numpy as jnp
from jax import lax
from jax.experimental import pallas as pl
from jax.experimental.pallas import tpu as pltpu
from jax.sharding import PartitionSpec as P

QUERIES = 256
GROUP = 16
WINDOW = 96
ALIGN = 16
LANES = 128
MESH = pl.DeviceIdType.MESH


def project_kernel(nf, row_ref, col_ref, acts_ref, grads_ref, in_ref, out_ref, inner_ref, outer_ref, ids_ref, parts):
    i = pl.program_id(0)
    rank = in_ref.shape[1]
    local_rank = rank // nf
    block, tokens = acts_ref.shape[0], parts.shape[0]
    bf = jnp.bfloat16
    here = pl.ds(pl.multiple_of(i * block, block), block)
    for k, (x, w) in enumerate(((acts_ref, in_ref), (grads_ref, out_ref))):
        part = jnp.dot(x[...], w[...], preferred_element_type=jnp.float32)
        high = part.astype(bf)
        parts[here, k * rank:(k + 1) * rank] = high
        parts[here, (2 + k) * rank:(3 + k) * rank] = (part - high.astype(jnp.float32)).astype(bf)

    @pl.when(i == pl.num_programs(0) - 1)
    def _():
        owners = row_ref[...]
        key = owners * tokens + lax.broadcasted_iota(jnp.int32, (1, tokens), 1)
        line = lax.broadcasted_iota(jnp.int32, (LANES, 1), 0)
        place = jnp.zeros((1, tokens), jnp.int32)
        for c in range(tokens // LANES):
            other = col_ref[c * LANES:(c + 1) * LANES, :] * tokens + (line + c * LANES)
            place += jnp.sum(jnp.where(other < key, 1, 0), axis=0, keepdims=True)
        names = owners.astype(jnp.float32)
        for c in range(tokens // LANES):
            rows = slice(c * LANES, (c + 1) * LANES)
            hits = place == line + c * LANES
            both = jnp.dot(jnp.where(hits, 1.0, 0.0).astype(bf), parts[...], preferred_element_type=jnp.float32)
            inner_ref[rows, :] = both[:, :rank] + both[:, 2 * rank:3 * rank]
            ids_ref[rows, :] = jnp.sum(jnp.where(hits, names, 0.0), axis=1, keepdims=True)
            for d in range(nf):
                pieces = [both[:, k * rank + d * local_rank:k * rank + (d + 1) * local_rank] for k in (1, 3)]
                rest = outer_ref.shape[2] - 2 * local_rank
                if rest:
                    pieces.append(jnp.zeros((LANES, rest), jnp.float32))
                outer_ref[d, rows, :] = jnp.concatenate(pieces, 1).astype(bf)


def exchange_kernel(nr, nf, local_rank, inner_ref, outer_ref, ids_ref, in_all, out_all,
                    rin, rout, far_in, far_out, to_in, to_out, rs_send, rs_recv, far_send, far_recv,
                    ring_send, ring_recv, f_send, f_recv, g_send, g_recv):
    row = lax.axis_index("rows")
    me = lax.axis_index("feat")
    tq, wide = rin.shape[1], rout.shape[2]
    odd = lax.rem(row, 2)
    pos = (1 - odd) * (row // 2) + odd * (nr - 1 - row // 2)

    def row_at(p):
        p = lax.rem(p + 2 * nr, nr)
        back = p // (nr // 2)
        return (1 - back) * (2 * p) + back * (2 * (nr - 1 - p) + 1)

    right, left = row_at(pos + 1), row_at(pos - 1)
    core = me + 1 - 2 * lax.rem(me, 2)
    half = nf // 2

    barrier = pltpu.get_barrier_semaphore()
    for d in range(1, half):
        pl.semaphore_signal(barrier, inc=1, device_id=(row, lax.rem(me + 2 * d, nf)), device_id_type=MESH)
    pl.semaphore_signal(barrier, inc=1, device_id=(row, core), device_id_type=MESH)
    for r in (right, left):
        pl.semaphore_signal(barrier, inc=1, device_id=(r, me), device_id_type=MESH)
    pl.semaphore_wait(barrier, half + 2)

    def remote(src, dst, ssem, rsem, dev):
        return pltpu.make_async_remote_copy(
            src_ref=src, dst_ref=dst, send_sem=ssem, recv_sem=rsem, device_id=dev, device_id_type=MESH)

    sends = []

    def begin(*args):
        c = remote(*args)
        c.start()
        sends.append(c)
        return c

    lane = lax.broadcasted_iota(jnp.int32, (1, wide), 1)

    def unpack(packed):
        both = packed.astype(jnp.float32)
        return both + pltpu.roll(both, wide - local_rank, 1)

    def pack(total):
        high = total.astype(jnp.bfloat16).astype(jnp.float32)
        low = pltpu.roll(total - high, local_rank, 1)
        return jnp.where(lane < local_rank, high, low).astype(jnp.bfloat16)

    near = {}
    for d in list(range(1, half)) + [0]:
        to = lax.rem(core + 2 * d, nf)
        near[d] = (begin(inner_ref.at[to], rin.at[d], rs_send.at[0, d], rs_recv.at[0, d], (row, core)),
                   begin(outer_ref.at[to], rout.at[d], rs_send.at[1, d], rs_recv.at[1, d], (row, core)))
    far = {}
    for d in range(1, half):
        to = lax.rem(me + 2 * d, nf)
        near[d][0].wait_recv()
        to_in[d - 1] = inner_ref[to] + rin[d]
        one = begin(to_in.at[d - 1], far_in.at[d - 1], far_send.at[0, d], far_recv.at[0, d], (row, to))
        near[d][1].wait_recv()
        to_out[d - 1] = pack(unpack(outer_ref[to]) + unpack(rout[d]))
        two = begin(to_out.at[d - 1], far_out.at[d - 1], far_send.at[1, d], far_recv.at[1, d], (row, to))
        far[d] = (one, two)
    mine = pl.ds(pl.multiple_of(me * tq, tq), tq)
    near[0][0].wait_recv()
    total = inner_ref[me] + rin[0]
    for d in range(1, half):
        far[d][0].wait_recv()
        total += far_in[d - 1]
    in_all[row, mine, :] = total.astype(jnp.bfloat16)
    near[0][1].wait_recv()
    total = unpack(outer_ref[me]) + unpack(rout[0])
    for d in range(1, half):
        far[d][1].wait_recv()
        total += unpack(far_out[d - 1])
    total = jnp.where(lane < local_rank, total, jnp.where(lane == local_rank, ids_ref[...], 0.0))
    out_all[row] = total.astype(jnp.bfloat16)

    steps_r = nr // 2
    steps_l = nr - 1 - steps_r

    def chunk_row(e):
        return row_at(pos - e) if e <= steps_r else row_at(pos + e - steps_r)

    def ring_copy(e, to, sem, w):
        r = chunk_row(e)
        block = out_all.at[r] if w else in_all.at[r, mine]
        return remote(block, block, ring_send.at[w, sem], ring_recv.at[w, sem], (to, me))

    def launch(e, to, sem, which=(0, 1)):
        pair = [ring_copy(e, to, sem, w) for w in which]
        for c in pair:
            c.start()
            sends.append(c)
        return pair

    tails = []
    feats = {}

    def spread(e):
        r = chunk_row(e)
        block = in_all.at[r, mine]
        got = []
        for d in range(1, half):
            c = remote(block, block, f_send.at[e, d], f_recv.at[e, d], (row, lax.rem(me + 2 * d, nf)))
            c.start()
            sends.append(c)
            got.append(c)
        c = remote(block, block, f_send.at[e, 0], f_recv.at[e, 0], (row, core))
        c.start()
        sends.append(c)
        tails.append(c)
        feats[e] = got

    def pass_on(e):
        r = chunk_row(e)
        for d in range(1, half):
            feats[e][d - 1].wait_recv()
            src = lax.rem(me + nf - 2 * d, nf)
            block = in_all.at[r, pl.ds(pl.multiple_of(src * tq, tq), tq)]
            c = remote(block, block, g_send.at[e, d], g_recv.at[e, d], (row, core))
            c.start()
            sends.append(c)
            tails.append(c)

    cr = launch(0, right, 0)
    cl = launch(0, left, steps_r)
    spread(0)
    late = [0]
    for s in range(steps_r):
        e = 1 + s
        fresh = [e]
        for c in cr:
            c.wait_recv()
        if s + 1 < steps_r:
            cr = launch(e, right, s + 1, (0, 1) if s + 2 < steps_r else (0,))
        spread(e)
        for c in cl:
            c.wait_recv()
        if s < steps_l:
            e = 1 + steps_r + s
            cl = launch(e, left, steps_r + s + 1, (0, 1) if s + 1 < steps_l else (1,))
            spread(e)
            fresh.append(e)
        for e in late:
            pass_on(e)
        late = fresh
    for e in late:
        pass_on(e)
    for c in tails:
        c.wait_recv()
    for c in sends:
        c.wait_send()


def total_kernel(nf, terms_ref, out_ref, got, send, recv):
    row = lax.axis_index("rows")
    me = lax.axis_index("feat")
    count = out_ref.shape[0]
    barrier = pltpu.get_barrier_semaphore()
    for d in range(1, nf):
        pl.semaphore_signal(barrier, inc=1, device_id=(row, lax.rem(me + d, nf)), device_id_type=MESH)
    pl.semaphore_wait(barrier, nf - 1)
    copies = []
    for d in range(1, nf):
        to = lax.rem(me + d, nf)
        c = pltpu.make_async_remote_copy(
            src_ref=terms_ref.at[pl.ds(pl.multiple_of(to * count, count), count)], dst_ref=got.at[d - 1],
            send_sem=send.at[d - 1], recv_sem=recv.at[d - 1], device_id=(row, to), device_id_type=MESH)
        c.start()
        copies.append(c)
    total = terms_ref[pl.ds(pl.multiple_of(me * count, count), count), :]
    for d in range(1, nf):
        copies[d - 1].wait_recv()
        total += got[d - 1]
    out_ref[...] = total
    for c in copies:
        c.wait_send()


def group_grads(g, starts_ref, inner_ref, outer_ref, scales_ref, held, in_w, out_w, acc):
    nr, tokens, rank = inner_ref.shape
    local_rank = scales_ref.shape[0]
    begins = []
    loops = jnp.int32(1)
    for r in range(nr):
        begin = starts_ref[r, g] // ALIGN * ALIGN
        begins.append(begin)
        loops = jnp.maximum(loops, (starts_ref[r, g + 1] - begin + WINDOW - 1) // WINDOW)
    acc[...] = jnp.zeros_like(acc)
    ids_here = (g * GROUP + lax.broadcasted_iota(jnp.int32, (GROUP, 1), 0)).astype(jnp.float32)
    line = lax.broadcasted_iota(jnp.int32, (WINDOW, 1), 0)

    def one(k, carry):
        for r in range(nr):
            want = begins[r] + k * WINDOW
            at = pl.multiple_of(jnp.minimum(want, tokens - WINDOW), ALIGN)
            here = pl.ds(r * WINDOW, WINDOW)
            in_w[here, :] = inner_ref[r, pl.ds(at, WINDOW), :]
            rows = outer_ref[r, pl.ds(at, WINDOW), :].astype(jnp.float32)
            out_w[here, :] = jnp.where(line >= want - at, rows, 0.0)
        turned = out_w[...].T
        mask = turned[local_rank:local_rank + 1, :] == ids_here
        spread = jnp.where(mask[None], turned[:local_rank, None, :], 0.0).astype(jnp.bfloat16)
        spread = spread.reshape(local_rank * GROUP, in_w.shape[0])
        acc[...] += jnp.dot(spread, in_w[...], preferred_element_type=jnp.float32)
        return carry

    lax.fori_loop(0, loops, one, 0)
    grads = acc[...].reshape(local_rank, GROUP, rank)
    scaled = (grads * scales_ref[...][:, None, :]).astype(jnp.bfloat16)
    held[:, pl.ds(pl.multiple_of(g * GROUP, GROUP), GROUP), :] = scaled


def score_kernel(step, starts_ref, inner_ref, outer_ref, scales_ref, codes_ref, zero_ref, out_ref,
                 in_w, out_w, acc, held):
    g = pl.program_id(0)
    groups = QUERIES // GROUP

    @pl.when(g < groups)
    def _():
        group_grads(g, starts_ref, inner_ref, outer_ref, scales_ref, held, in_w, out_w, acc)

    @pl.when(g == groups)
    def _():
        out_ref[...] = jnp.zeros_like(out_ref)

    @pl.when(g >= groups)
    def _():
        width = held.shape[2]
        total = out_ref[...]
        for i in range(step):
            cols = slice(i * width, (i + 1) * width)
            levels = (codes_ref[:, cols] - zero_ref[:, cols]).astype(jnp.float32).astype(jnp.bfloat16)
            total += lax.dot_general(held[(g - groups) * step + i], levels, (((1,), (1,)), ((), ())),
                                     preferred_element_type=jnp.float32)
        out_ref[...] = total


def local(nr, nf, acts, out_grads, proj_in, proj_out, assignment, codes, zero_points, scales):
    tokens = acts.shape[0]
    rank = proj_in.shape[1]
    local_rank = rank // nf
    bf = jnp.bfloat16
    vmem = pl.BlockSpec(memory_space=pltpu.VMEM)
    dma = pltpu.SemaphoreType.DMA
    wide = -(-2 * local_rank // LANES) * LANES
    block = tokens // 4
    inner, outer, ids = pl.pallas_call(
        functools.partial(project_kernel, nf),
        out_shape=(jax.ShapeDtypeStruct((tokens, rank), jnp.float32),
                   jax.ShapeDtypeStruct((nf, tokens, wide), bf),
                   jax.ShapeDtypeStruct((tokens, 1), jnp.float32)),
        grid=(4,),
        in_specs=[vmem, vmem,
                  pl.BlockSpec((block, acts.shape[1]), lambda i: (i, 0)),
                  pl.BlockSpec((block, acts.shape[1]), lambda i: (i, 0)),
                  vmem, vmem],
        out_specs=(vmem, vmem, vmem),
        scratch_shapes=[pltpu.VMEM((tokens, 4 * rank), bf)],
        compiler_params=pltpu.CompilerParams(vmem_limit_bytes=40 * 2 ** 20),
    )(assignment[None, :], assignment[:, None], acts, out_grads, proj_in, proj_out)
    inner = inner.reshape(nf, tokens // nf, rank)
    in_all, out_all = pl.pallas_call(
        functools.partial(exchange_kernel, nr, nf, local_rank),
        out_shape=(jax.ShapeDtypeStruct((nr, tokens, rank), bf), jax.ShapeDtypeStruct((nr, tokens, wide), bf)),
        in_specs=[vmem, vmem, vmem],
        out_specs=(vmem, vmem),
        scratch_shapes=[
            pltpu.VMEM((nf // 2, tokens // nf, rank), jnp.float32),
            pltpu.VMEM((nf // 2, tokens, wide), bf),
            pltpu.VMEM((nf // 2 - 1, tokens // nf, rank), jnp.float32),
            pltpu.VMEM((nf // 2 - 1, tokens, wide), bf),
            pltpu.VMEM((nf // 2 - 1, tokens // nf, rank), jnp.float32),
            pltpu.VMEM((nf // 2 - 1, tokens, wide), bf),
            dma((2, nf // 2)), dma((2, nf // 2)),
            dma((2, nf // 2)), dma((2, nf // 2)),
            dma((2, nr)), dma((2, nr)),
            dma((nr, nf // 2)), dma((nr, nf // 2)),
            dma((nr, nf // 2)), dma((nr, nf // 2)),
        ],
        compiler_params=pltpu.CompilerParams(
            collective_id=0, has_side_effects=True, vmem_limit_bytes=48 * 2 ** 20),
    )(inner, outer, ids)
    edges = lax.iota(jnp.int32, QUERIES // GROUP + 1) * GROUP
    found = out_all[:, :, local_rank].astype(jnp.int32)
    starts = jnp.sum((found[:, None, :] < edges[None, :, None]).astype(jnp.int32), axis=2)

    stored, features = codes.shape
    step = min(8, local_rank)
    groups = QUERIES // GROUP
    terms = pl.pallas_call(
        functools.partial(score_kernel, step),
        out_shape=jax.ShapeDtypeStruct((QUERIES, stored), jnp.float32),
        grid=(groups + local_rank // step,),
        in_specs=[
            pl.BlockSpec(memory_space=pltpu.SMEM), vmem, vmem, vmem,
            pl.BlockSpec((stored, step * rank), lambda i: (0, jnp.maximum(i - groups, 0))),
            pl.BlockSpec((1, step * rank), lambda i: (0, jnp.maximum(i - groups, 0))),
        ],
        out_specs=vmem,
        scratch_shapes=[
            pltpu.VMEM((nr * WINDOW, rank), bf),
            pltpu.VMEM((nr * WINDOW, wide), jnp.float32),
            pltpu.VMEM((local_rank * GROUP, rank), jnp.float32),
            pltpu.VMEM((local_rank, QUERIES, rank), bf),
        ],
        compiler_params=pltpu.CompilerParams(vmem_limit_bytes=56 * 2 ** 20),
    )(starts, in_all, out_all, scales.reshape(local_rank, rank), codes, zero_points.reshape(1, features))
    return pl.pallas_call(
        functools.partial(total_kernel, nf),
        out_shape=jax.ShapeDtypeStruct((QUERIES // nf, stored), jnp.float32),
        in_specs=[vmem],
        out_specs=vmem,
        scratch_shapes=[pltpu.VMEM((nf - 1, QUERIES // nf, stored), jnp.float32), dma((nf - 1,)), dma((nf - 1,))],
        compiler_params=pltpu.CompilerParams(collective_id=1, has_side_effects=True),
    )(terms)


def solution(mesh):
    in_specs = (
        P("rows", "feat"),
        P("rows", "feat"),
        P("feat", None),
        P("feat", None),
        P("rows"),
        P("rows", "feat"),
        P("feat"),
        P("feat"),
    )
    out_specs = P("feat", "rows")
    body = functools.partial(local, mesh.shape["rows"], mesh.shape["feat"])
    return jax.shard_map(body, mesh=mesh, in_specs=in_specs, out_specs=out_specs, check_vma=False)
```

```python
import functools
import jax
import jax.numpy as jnp
from jax import lax
from jax.experimental import pallas as pl
from jax.experimental.pallas import tpu as pltpu
from jax.sharding import PartitionSpec as P

QUERIES = 256
GROUP = 16
WINDOW = 96
ALIGN = 16
LANES = 128
MESH = pl.DeviceIdType.MESH


def project_kernel(nf, row_ref, col_ref, acts_ref, grads_ref, in_ref, out_ref, inner_ref, outer_ref, ids_ref, parts):
    i = pl.program_id(0)
    rank = in_ref.shape[1]
    local_rank = rank // nf
    block, tokens = acts_ref.shape[0], parts.shape[0]
    bf = jnp.bfloat16
    here = pl.ds(pl.multiple_of(i * block, block), block)
    for k, (x, w) in enumerate(((acts_ref, in_ref), (grads_ref, out_ref))):
        part = jnp.dot(x[...], w[...], preferred_element_type=jnp.float32)
        high = part.astype(bf)
        parts[here, k * rank:(k + 1) * rank] = high
        parts[here, (2 + k) * rank:(3 + k) * rank] = (part - high.astype(jnp.float32)).astype(bf)

    @pl.when(i == pl.num_programs(0) - 1)
    def _():
        owners = row_ref[...]
        key = owners * tokens + lax.broadcasted_iota(jnp.int32, (1, tokens), 1)
        line = lax.broadcasted_iota(jnp.int32, (LANES, 1), 0)
        place = jnp.zeros((1, tokens), jnp.int32)
        for c in range(tokens // LANES):
            other = col_ref[c * LANES:(c + 1) * LANES, :] * tokens + (line + c * LANES)
            place += jnp.sum(jnp.where(other < key, 1, 0), axis=0, keepdims=True)
        names = owners.astype(jnp.float32)
        for c in range(tokens // LANES):
            rows = slice(c * LANES, (c + 1) * LANES)
            hits = place == line + c * LANES
            both = jnp.dot(jnp.where(hits, 1.0, 0.0).astype(bf), parts[...], preferred_element_type=jnp.float32)
            inner_ref[rows, :] = both[:, :rank] + both[:, 2 * rank:3 * rank]
            ids_ref[rows, :] = jnp.sum(jnp.where(hits, names, 0.0), axis=1, keepdims=True)
            for d in range(nf):
                pieces = [both[:, k * rank + d * local_rank:k * rank + (d + 1) * local_rank] for k in (1, 3)]
                rest = outer_ref.shape[2] - 2 * local_rank
                if rest:
                    pieces.append(jnp.zeros((LANES, rest), jnp.float32))
                outer_ref[d, rows, :] = jnp.concatenate(pieces, 1).astype(bf)


def exchange_kernel(nr, nf, local_rank, inner_ref, outer_ref, ids_ref, in_all, out_all,
                    rin, rout, far_in, far_out, to_in, to_out, rs_send, rs_recv, far_send, far_recv,
                    ring_send, ring_recv, f_send, f_recv, g_send, g_recv):
    row = lax.axis_index("rows")
    me = lax.axis_index("feat")
    tq, wide = rin.shape[1], rout.shape[2]
    odd = lax.rem(row, 2)
    pos = (1 - odd) * (row // 2) + odd * (nr - 1 - row // 2)

    def row_at(p):
        p = lax.rem(p + 2 * nr, nr)
        back = p // (nr // 2)
        return (1 - back) * (2 * p) + back * (2 * (nr - 1 - p) + 1)

    right, left = row_at(pos + 1), row_at(pos - 1)
    core = me + 1 - 2 * lax.rem(me, 2)
    half = nf // 2

    barrier = pltpu.get_barrier_semaphore()
    for d in range(1, half):
        pl.semaphore_signal(barrier, inc=1, device_id=(row, lax.rem(me + 2 * d, nf)), device_id_type=MESH)
    pl.semaphore_signal(barrier, inc=1, device_id=(row, core), device_id_type=MESH)
    for r in (right, left):
        pl.semaphore_signal(barrier, inc=1, device_id=(r, me), device_id_type=MESH)
    pl.semaphore_wait(barrier, half + 2)

    def remote(src, dst, ssem, rsem, dev):
        return pltpu.make_async_remote_copy(
            src_ref=src, dst_ref=dst, send_sem=ssem, recv_sem=rsem, device_id=dev, device_id_type=MESH)

    sends = []

    def begin(*args):
        c = remote(*args)
        c.start()
        sends.append(c)
        return c

    lane = lax.broadcasted_iota(jnp.int32, (1, wide), 1)

    def unpack(packed):
        both = packed.astype(jnp.float32)
        return both + pltpu.roll(both, wide - local_rank, 1)

    def pack(total):
        high = total.astype(jnp.bfloat16).astype(jnp.float32)
        low = pltpu.roll(total - high, local_rank, 1)
        return jnp.where(lane < local_rank, high, low).astype(jnp.bfloat16)

    near = {}
    turns = list(range(1, half)) + [0]
    for w, src, dst in ((0, inner_ref, rin), (1, outer_ref, rout)):
        for d in turns:
            to = lax.rem(core + 2 * d, nf)
            near[d, w] = begin(src.at[to], dst.at[d], rs_send.at[w, d], rs_recv.at[w, d], (row, core))
    far = {}
    for d in range(1, half):
        to = lax.rem(me + 2 * d, nf)
        near[d, 0].wait_recv()
        to_in[d - 1] = inner_ref[to] + rin[d]
        far[d, 0] = begin(to_in.at[d - 1], far_in.at[d - 1], far_send.at[0, d], far_recv.at[0, d], (row, to))
    for d in range(1, half):
        to = lax.rem(me + 2 * d, nf)
        near[d, 1].wait_recv()
        to_out[d - 1] = pack(unpack(outer_ref[to]) + unpack(rout[d]))
        far[d, 1] = begin(to_out.at[d - 1], far_out.at[d - 1], far_send.at[1, d], far_recv.at[1, d], (row, to))
    mine = pl.ds(pl.multiple_of(me * tq, tq), tq)
    near[0, 0].wait_recv()
    total = inner_ref[me] + rin[0]
    for d in range(1, half):
        far[d, 0].wait_recv()
        total += far_in[d - 1]
    in_all[row, mine, :] = total.astype(jnp.bfloat16)
    steps_r = nr // 2
    steps_l = nr - 1 - steps_r

    def chunk_row(e):
        return row_at(pos - e) if e <= steps_r else row_at(pos + e - steps_r)

    def ring_copy(e, to, sem, w):
        r = chunk_row(e)
        block = out_all.at[r] if w else in_all.at[r, mine]
        return remote(block, block, ring_send.at[w, sem], ring_recv.at[w, sem], (to, me))

    def launch(e, to, sem, which=(0, 1)):
        pair = [ring_copy(e, to, sem, w) for w in which]
        for c in pair:
            c.start()
            sends.append(c)
        return pair

    tails = []
    feats = {}

    def spread(e):
        r = chunk_row(e)
        block = in_all.at[r, mine]
        got = []
        for d in range(1, half):
            c = remote(block, block, f_send.at[e, d], f_recv.at[e, d], (row, lax.rem(me + 2 * d, nf)))
            c.start()
            sends.append(c)
            got.append(c)
        c = remote(block, block, f_send.at[e, 0], f_recv.at[e, 0], (row, core))
        c.start()
        sends.append(c)
        tails.append(c)
        feats[e] = got

    def pass_on(e):
        r = chunk_row(e)
        for d in range(1, half):
            feats[e][d - 1].wait_recv()
            src = lax.rem(me + nf - 2 * d, nf)
            block = in_all.at[r, pl.ds(pl.multiple_of(src * tq, tq), tq)]
            c = remote(block, block, g_send.at[e, d], g_recv.at[e, d], (row, core))
            c.start()
            sends.append(c)
            tails.append(c)

    cr = launch(0, right, 0, (0,))
    cl = launch(0, left, steps_r, (0,))
    spread(0)
    near[0, 1].wait_recv()
    total = unpack(outer_ref[me]) + unpack(rout[0])
    for d in range(1, half):
        far[d, 1].wait_recv()
        total += unpack(far_out[d - 1])
    total = jnp.where(lane < local_rank, total, jnp.where(lane == local_rank, ids_ref[...], 0.0))
    out_all[row] = total.astype(jnp.bfloat16)
    dr = launch(0, right, 0, (1,))
    dl = launch(0, left, steps_r, (1,))
    late = [0]
    for s in range(steps_r):
        e, el = 1 + s, 1 + steps_r + s
        fresh = [e]
        for c in cr:
            c.wait_recv()
        if s + 1 < steps_r:
            cr = launch(e, right, s + 1, (0,))
        spread(e)
        if s < steps_l:
            for c in cl:
                c.wait_recv()
            cl = launch(el, left, el, (0,)) if s + 1 < steps_l else []
            spread(el)
            fresh.append(el)
        for c in dr:
            c.wait_recv()
        dr = launch(e, right, s + 1, (1,)) if s + 2 < steps_r else []
        for c in dl:
            c.wait_recv()
        if s < steps_l:
            dl = launch(el, left, el, (1,))
        for e in late:
            pass_on(e)
        late = fresh
    for e in late:
        pass_on(e)
    for c in tails:
        c.wait_recv()
    for c in sends:
        c.wait_send()


def total_kernel(nf, terms_ref, out_ref, got, send, recv):
    row = lax.axis_index("rows")
    me = lax.axis_index("feat")
    count = out_ref.shape[0]
    barrier = pltpu.get_barrier_semaphore()
    for d in range(1, nf):
        pl.semaphore_signal(barrier, inc=1, device_id=(row, lax.rem(me + d, nf)), device_id_type=MESH)
    pl.semaphore_wait(barrier, nf - 1)
    copies = []
    for d in range(1, nf):
        to = lax.rem(me + d, nf)
        c = pltpu.make_async_remote_copy(
            src_ref=terms_ref.at[pl.ds(pl.multiple_of(to * count, count), count)], dst_ref=got.at[d - 1],
            send_sem=send.at[d - 1], recv_sem=recv.at[d - 1], device_id=(row, to), device_id_type=MESH)
        c.start()
        copies.append(c)
    total = terms_ref[pl.ds(pl.multiple_of(me * count, count), count), :]
    for d in range(1, nf):
        copies[d - 1].wait_recv()
        total += got[d - 1]
    out_ref[...] = total
    for c in copies:
        c.wait_send()


def group_grads(g, starts_ref, inner_ref, outer_ref, scales_ref, held, in_w, out_w, acc):
    nr, tokens, rank = inner_ref.shape
    local_rank = scales_ref.shape[0]
    begins = []
    loops = jnp.int32(1)
    for r in range(nr):
        begin = starts_ref[r, g] // ALIGN * ALIGN
        begins.append(begin)
        loops = jnp.maximum(loops, (starts_ref[r, g + 1] - begin + WINDOW - 1) // WINDOW)
    acc[...] = jnp.zeros_like(acc)
    ids_here = (g * GROUP + lax.broadcasted_iota(jnp.int32, (GROUP, 1), 0)).astype(jnp.float32)
    line = lax.broadcasted_iota(jnp.int32, (WINDOW, 1), 0)

    def one(k, carry):
        for r in range(nr):
            want = begins[r] + k * WINDOW
            at = pl.multiple_of(jnp.minimum(want, tokens - WINDOW), ALIGN)
            here = pl.ds(r * WINDOW, WINDOW)
            in_w[here, :] = inner_ref[r, pl.ds(at, WINDOW), :]
            rows = outer_ref[r, pl.ds(at, WINDOW), :].astype(jnp.float32)
            out_w[here, :] = jnp.where(line >= want - at, rows, 0.0)
        turned = out_w[...].T
        mask = turned[local_rank:local_rank + 1, :] == ids_here
        spread = jnp.where(mask[None], turned[:local_rank, None, :], 0.0).astype(jnp.bfloat16)
        spread = spread.reshape(local_rank * GROUP, in_w.shape[0])
        acc[...] += jnp.dot(spread, in_w[...], preferred_element_type=jnp.float32)
        return carry

    lax.fori_loop(0, loops, one, 0)
    grads = acc[...].reshape(local_rank, GROUP, rank)
    scaled = (grads * scales_ref[...][:, None, :]).astype(jnp.bfloat16)
    held[:, pl.ds(pl.multiple_of(g * GROUP, GROUP), GROUP), :] = scaled


def score_kernel(step, starts_ref, inner_ref, outer_ref, scales_ref, codes_ref, zero_ref, out_ref,
                 in_w, out_w, acc, held):
    g = pl.program_id(0)
    groups = QUERIES // GROUP

    @pl.when(g < groups)
    def _():
        group_grads(g, starts_ref, inner_ref, outer_ref, scales_ref, held, in_w, out_w, acc)

    @pl.when(g == groups)
    def _():
        out_ref[...] = jnp.zeros_like(out_ref)

    @pl.when(g >= groups)
    def _():
        width = held.shape[2]
        total = out_ref[...]
        for i in range(step):
            cols = slice(i * width, (i + 1) * width)
            levels = (codes_ref[:, cols] - zero_ref[:, cols]).astype(jnp.float32).astype(jnp.bfloat16)
            total += lax.dot_general(held[(g - groups) * step + i], levels, (((1,), (1,)), ((), ())),
                                     preferred_element_type=jnp.float32)
        out_ref[...] = total


def local(nr, nf, acts, out_grads, proj_in, proj_out, assignment, codes, zero_points, scales):
    tokens = acts.shape[0]
    rank = proj_in.shape[1]
    local_rank = rank // nf
    bf = jnp.bfloat16
    vmem = pl.BlockSpec(memory_space=pltpu.VMEM)
    dma = pltpu.SemaphoreType.DMA
    wide = -(-2 * local_rank // LANES) * LANES
    block = tokens // 4
    inner, outer, ids = pl.pallas_call(
        functools.partial(project_kernel, nf),
        out_shape=(jax.ShapeDtypeStruct((tokens, rank), jnp.float32),
                   jax.ShapeDtypeStruct((nf, tokens, wide), bf),
                   jax.ShapeDtypeStruct((tokens, 1), jnp.float32)),
        grid=(4,),
        in_specs=[vmem, vmem,
                  pl.BlockSpec((block, acts.shape[1]), lambda i: (i, 0)),
                  pl.BlockSpec((block, acts.shape[1]), lambda i: (i, 0)),
                  vmem, vmem],
        out_specs=(vmem, vmem, vmem),
        scratch_shapes=[pltpu.VMEM((tokens, 4 * rank), bf)],
        compiler_params=pltpu.CompilerParams(vmem_limit_bytes=56 * 2 ** 20),
    )(assignment[None, :], assignment[:, None], acts, out_grads, proj_in, proj_out)
    inner = inner.reshape(nf, tokens // nf, rank)
    in_all, out_all = pl.pallas_call(
        functools.partial(exchange_kernel, nr, nf, local_rank),
        out_shape=(jax.ShapeDtypeStruct((nr, tokens, rank), bf), jax.ShapeDtypeStruct((nr, tokens, wide), bf)),
        in_specs=[vmem, vmem, vmem],
        out_specs=(vmem, vmem),
        scratch_shapes=[
            pltpu.VMEM((nf // 2, tokens // nf, rank), jnp.float32),
            pltpu.VMEM((nf // 2, tokens, wide), bf),
            pltpu.VMEM((nf // 2 - 1, tokens // nf, rank), jnp.float32),
            pltpu.VMEM((nf // 2 - 1, tokens, wide), bf),
            pltpu.VMEM((nf // 2 - 1, tokens // nf, rank), jnp.float32),
            pltpu.VMEM((nf // 2 - 1, tokens, wide), bf),
            dma((2, nf // 2)), dma((2, nf // 2)),
            dma((2, nf // 2)), dma((2, nf // 2)),
            dma((2, nr)), dma((2, nr)),
            dma((nr, nf // 2)), dma((nr, nf // 2)),
            dma((nr, nf // 2)), dma((nr, nf // 2)),
        ],
        compiler_params=pltpu.CompilerParams(
            collective_id=0, has_side_effects=True, vmem_limit_bytes=48 * 2 ** 20),
    )(inner, outer, ids)
    edges = lax.iota(jnp.int32, QUERIES // GROUP + 1) * GROUP
    found = out_all[:, :, local_rank].astype(jnp.int32)
    starts = jnp.sum((found[:, None, :] < edges[None, :, None]).astype(jnp.int32), axis=2)

    stored, features = codes.shape
    step = min(8, local_rank)
    groups = QUERIES // GROUP
    terms = pl.pallas_call(
        functools.partial(score_kernel, step),
        out_shape=jax.ShapeDtypeStruct((QUERIES, stored), jnp.float32),
        grid=(groups + local_rank // step,),
        in_specs=[
            pl.BlockSpec(memory_space=pltpu.SMEM), vmem, vmem, vmem,
            pl.BlockSpec((stored, step * rank), lambda i: (0, jnp.maximum(i - groups, 0))),
            pl.BlockSpec((1, step * rank), lambda i: (0, jnp.maximum(i - groups, 0))),
        ],
        out_specs=vmem,
        scratch_shapes=[
            pltpu.VMEM((nr * WINDOW, rank), bf),
            pltpu.VMEM((nr * WINDOW, wide), jnp.float32),
            pltpu.VMEM((local_rank * GROUP, rank), jnp.float32),
            pltpu.VMEM((local_rank, QUERIES, rank), bf),
        ],
        compiler_params=pltpu.CompilerParams(vmem_limit_bytes=56 * 2 ** 20),
    )(starts, in_all, out_all, scales.reshape(local_rank, rank), codes, zero_points.reshape(1, features))
    return pl.pallas_call(
        functools.partial(total_kernel, nf),
        out_shape=jax.ShapeDtypeStruct((QUERIES // nf, stored), jnp.float32),
        in_specs=[vmem],
        out_specs=vmem,
        scratch_shapes=[pltpu.VMEM((nf - 1, QUERIES // nf, stored), jnp.float32), dma((nf - 1,)), dma((nf - 1,))],
        compiler_params=pltpu.CompilerParams(collective_id=1, has_side_effects=True),
    )(terms)


def solution(mesh):
    in_specs = (
        P("rows", "feat"),
        P("rows", "feat"),
        P("feat", None),
        P("feat", None),
        P("rows"),
        P("rows", "feat"),
        P("feat"),
        P("feat"),
    )
    out_specs = P("feat", "rows")
    body = functools.partial(local, mesh.shape["rows"], mesh.shape["feat"])
    return jax.shard_map(body, mesh=mesh, in_specs=in_specs, out_specs=out_specs, check_vma=False)
```
